32 devices in a mesh: clip: 2 (over y), row: 4 (over z), col: 2 (over x), pol: 2 (over core).
Axes of the slice: x: 2, y: 2, z: 4, core: 2. Of those that a mesh axis runs over, the one named last changes fastest.
Arguments:
- tcc_blocks: bfloat16 [8, 2, 2, 16, 2, 256, 256], P(('clip', 'row'), 'col', 'pol'), parts along dimension 0, may hold values from -32 to 32
- slot_rows: int32 [8, 2, 2, 16], P(('clip', 'row'), 'col', 'pol'), parts along dimension 0, may hold values from 0 to 3, as said below
- slot_cols: int32 [8, 2, 2, 16], P(('clip', 'row'), 'col', 'pol'), parts along dimension 0, may hold values from 0 to 3
- slot_count: int32 [8, 2, 2], P(('clip', 'row'), 'col', 'pol'), parts along dimension 0, may hold values from 1 to 16, as said below
- subspace: bfloat16 [8192, 256], P(('clip', 'row', 'col', 'pol')), parts along dimension 0, may hold values from -6 to 6
Outputs:
- subspace_out: float32 [8192, 256], P(('clip', 'row', 'col', 'pol')), parts along dimension 0
- gram_factor: float32 [256, 128], P('clip'), parts along dimension 0
The draws below stay inside these ranges and needn't reach their ends.
There are 2 independent parts, one for each index of `clip`. The reference program is written for one: setup_inputs(seed, part) draws one part's arguments, and reference() takes and returns one part's arrays. A program takes and returns all parts, laid end to end along the dimension named above; each array names one. Nothing has to cross between parts.
Inputs may be any that keep to these rules, and one draw needn't show every extreme that they name: Within one device position the pairs of slot_rows and slot_cols of all 16 slots are distinct. `slot_count`: some device position has all 16 slots live.
All inputs are finite; a program needn't handle non-finite values.
Results may differ from the reference program's by a relative error of at most 0.003.
Values may be sent and summed in bfloat16 or wider, within the bound.
A program may use at most 64 MiB of HBM per device.

```python
import jax
import jax.numpy as jnp
from jax import lax

BS = 256
K = 128
SLOTS = 16
ITERS = 2
NORD = 4096
N_ROW = 4
N_COL = 2
N_POL = 2


def structure(key):
    col_group = N_COL * N_POL
    devices = N_ROW * col_group
    places = col_group * N_ROW
    scores = jax.random.randint(jax.random.fold_in(key, 101), (devices, places), 0, 1 << 20, dtype=jnp.int32) * places + jnp.arange(places, dtype=jnp.int32)[None, :]
    chosen = jnp.argsort(scores, axis=1, stable=True)[:, :SLOTS].astype(jnp.int32)
    row_ids = chosen // N_ROW
    col_ids = chosen % N_ROW
    base_count = jax.random.randint(jax.random.fold_in(key, 102), (devices,), max(SLOTS // 4, 1), SLOTS // 2 + 1, dtype=jnp.int32)
    heavy = jax.random.randint(jax.random.fold_in(key, 103), (devices,), 0, 4, dtype=jnp.int32) == 0
    forced = jnp.arange(devices, dtype=jnp.int32) == jax.random.randint(jax.random.fold_in(key, 104), (), 0, devices, dtype=jnp.int32)
    counts = jnp.where(heavy | forced, SLOTS, base_count).astype(jnp.int32)
    return (row_ids, col_ids, counts)


def draw_slot_rows(key, part):
    shared = structure(key)
    return shared[0].reshape(N_ROW, N_COL, N_POL, SLOTS)


def draw_slot_cols(key, part):
    shared = structure(key)
    return shared[1].reshape(N_ROW, N_COL, N_POL, SLOTS)


def draw_slot_count(key, part):
    shared = structure(key)
    return shared[2].reshape(N_ROW, N_COL, N_POL)


def draw_tcc_blocks(key, part):
    shared = structure(key)
    key = jax.random.fold_in(key, 11)
    col_group = N_COL * N_POL
    devices = N_ROW * col_group
    shape = (devices, SLOTS, 2, BS, BS)
    values = jax.random.truncated_normal(key, -4.0, 4.0, shape, jnp.float32)
    table = jax.random.uniform(jax.random.fold_in(key, 12), (NORD,), jnp.float32)
    tile_index = jnp.arange(devices, dtype=jnp.int32) // col_group
    block_row = tile_index[:, None] * col_group + shared[0]
    global_row = block_row[:, :, None] * BS + jnp.arange(BS, dtype=jnp.int32)[None, None, :]
    rise = global_row.astype(jnp.float32) / NORD
    scales = 10.0 ** table[global_row] * 3.0 ** rise
    values = values * scales[:, :, None, :, None] / jnp.sqrt(jnp.float32(SLOTS * BS // 2))
    return values.reshape(N_ROW, N_COL, N_POL, SLOTS, 2, BS, BS).astype(jnp.bfloat16)


def shard_levels(stream_key, shape, cuts, low, high):
    def one(position, blocks):
        steps = jax.random.uniform(jax.random.fold_in(jax.random.fold_in(stream_key, 6), position), (blocks,), jnp.float32, low / len(cuts), high / len(cuts))
        return jnp.repeat(jnp.exp(steps), shape[position] // blocks).reshape((-1,) + (1,) * (len(shape) - position - 1))

    factor_of = one(*cuts[0])
    for cut in cuts[1:]:
        factor_of = factor_of * one(*cut)
    return factor_of


def bell_draw(key, extent, scale, most, split=(), kind=jnp.bfloat16):
    gain = shard_levels(key, extent, split, -0.22, 0.18) if split else 1.0
    entries = jax.random.normal(key, extent, jnp.float32) * scale * gain
    return jnp.minimum(jnp.maximum(entries, -most), most).astype(kind)


def setup_inputs(seed: int = 0, part: int = 0) -> dict:
    streams_of = jax.random.split(jax.random.key(seed), 6)
    part_keys = jax.random.split(jax.random.fold_in(streams_of[5], part), 6)
    return {
        "tcc_blocks": draw_tcc_blocks(jax.random.fold_in(jax.random.fold_in(streams_of[5], part), 71), part),
        "slot_rows": draw_slot_rows(jax.random.fold_in(jax.random.fold_in(streams_of[5], part), 71), part),
        "slot_cols": draw_slot_cols(jax.random.fold_in(jax.random.fold_in(streams_of[5], part), 71), part),
        "slot_count": draw_slot_count(jax.random.fold_in(jax.random.fold_in(streams_of[5], part), 71), part),
        "subspace": bell_draw(part_keys[4], (NORD, 2 * K), 1.0, 6.0, ((0, 16),)),
    }


def reference(tcc_blocks, slot_rows, slot_cols, slot_count, subspace):
    col_group = N_COL * N_POL
    devices = N_ROW * col_group
    width_all = 2 * K
    blocks = tcc_blocks.reshape(devices, SLOTS, 2 * BS, BS)
    row_ids = slot_rows.reshape(devices, SLOTS).astype(jnp.int32)
    device_ids = jnp.arange(devices, dtype=jnp.int32)
    tile_rows = device_ids // col_group
    global_cols = (slot_cols.reshape(devices, SLOTS).astype(jnp.int32) * col_group + (device_ids % col_group)[:, None]).astype(jnp.int32)
    alive_mask = (jnp.arange(SLOTS, dtype=jnp.int32)[None, :] < slot_count.reshape(devices).astype(jnp.int32)[:, None]).astype(jnp.float32)
    targets = (row_ids[:, :, None] == jnp.arange(col_group, dtype=jnp.int32)[None, None, :]).astype(jnp.float32) * alive_mask[:, :, None]
    current = subspace
    for iteration in range(ITERS):
        panel_rows = current.reshape(devices, BS, width_all)

        def visit_device(running, pieces):
            block_data, columns, placing, tile_index = pieces
            picked = panel_rows[columns].astype(jnp.float32)
            product = jnp.einsum('sij,sjc->sic', block_data.astype(jnp.float32), picked, precision=lax.Precision.HIGHEST)
            real_part = product[:, :BS, :K] - product[:, BS:, K:]
            imag_part = product[:, :BS, K:] + product[:, BS:, :K]
            contribution = jnp.concatenate([real_part, imag_part], axis=2)
            tile_sum = jnp.einsum('st,sic->tic', placing, contribution, precision=lax.Precision.HIGHEST)
            begin_row = (tile_index * col_group).astype(jnp.int32)
            before = lax.dynamic_slice_in_dim(running, begin_row, col_group, 0)
            return (lax.dynamic_update_slice_in_dim(running, before + tile_sum, begin_row, 0), None)
        image, unused = lax.scan(visit_device, jnp.zeros((devices, BS, width_all), jnp.float32), (blocks, global_cols, targets, tile_rows))
        iterate = image.reshape(NORD, width_all)
        halves = iterate.reshape(NORD, 2, K)
        gram = jnp.einsum('nak,nal->kl', halves, halves, precision=lax.Precision.HIGHEST) / (2.0 * NORD)
        factor = jnp.linalg.cholesky(gram)
        solved = lax.linalg.triangular_solve(factor, iterate.reshape(2 * NORD, K), left_side=False, lower=True, transpose_a=True)
        orthonormal = solved.reshape(NORD, width_all)
        current = orthonormal.astype(jnp.bfloat16)
    return (orthonormal, factor)
```

```python
import functools

import jax
import jax.numpy as jnp
from jax import lax
from jax.experimental import pallas as pl
from jax.experimental.pallas import tpu as pltpu
from jax.sharding import PartitionSpec as P

ITERS = 2
F32 = jnp.float32
BF16 = jnp.bfloat16
HI = lax.Precision.HIGHEST
PANEL = 8


def factor_and_inverse(gram):
    order = gram.shape[0]
    lane = lax.broadcasted_iota(jnp.int32, (1, order), 1)
    lanes = lax.broadcasted_iota(jnp.int32, (PANEL, order), 1)
    subs = lax.broadcasted_iota(jnp.int32, (PANEL, order), 0)
    upper_rows, inverse_rows = [], []
    rest = gram
    for start in range(0, order, PANEL):
        top, rest = rest[:PANEL], rest[PANEL:]
        left = order - start - PANEL
        diag = [jnp.broadcast_to(top[:, start + k:start + k + 1], (PANEL, order)) for k in range(PANEL)]
        if left:
            below = [jnp.broadcast_to(rest[:, start + k:start + k + 1], (left, order)) for k in range(PANEL)]
            rest = jnp.where((lane >= start) & (lane < start + PANEL), 0.0, rest)
        pivots = diag[0]
        for k in range(PANEL):
            here = start + k
            inv = 1.0 / diag[k][k:k + 1]
            under = jnp.where(subs > k, diag[k], 0.0)
            mults = {l: diag[l][k:k + 1] * inv for l in range(k + 1, PANEL)}
            row = jnp.where(lane == here, 1.0, top[k:k + 1]) * inv
            if k:
                pivots = jnp.where(subs == k, diag[k], pivots)
            top = jnp.where((lanes == here) & (subs > k), 0.0, top) - under * row
            for l in range(k + 1, PANEL):
                diag[l] = diag[l] - under * mults[l]
            if left:
                row = jnp.where((lane > here) & (lane < start + PANEL), 0.0, row)
                rest = rest - below[k] * row
                for l in range(k + 1, PANEL):
                    below[l] = below[l] - below[k] * mults[l]
        root = lax.rsqrt(pivots)
        scaled = top * root
        upper_rows.append(jnp.where(lanes >= subs + start, scaled, 0.0))
        inverse_rows.append(jnp.where(lanes < subs + start, scaled, jnp.where(lanes == subs + start, root, 0.0)))
    return jnp.concatenate(upper_rows, axis=0), jnp.concatenate(inverse_rows, axis=0)


def kernel(
    sizes,
    blocks_hbm, rows_ref, cols_ref, count_ref, sub_ref,
    out_ref, factor_ref,
    blk, panel, weights, table, ctable, sums, own1, send1, recv1, send2, recv2, ybuf, ygather,
    gram_own, gram_a, gram_b, gram_sb, gram_full,
    blk_sem, p_send, p_recv, s1_send, s1_recv, s2_send, s2_recv, y_send, y_recv,
    a_send, a_recv, b_send, b_recv, c_send, c_recv,
):
    n_row, n_col, n_pol, slots, bs, width = sizes
    half = width // 2
    group = n_col * n_pol
    chunk = half // group
    scale = 1.0 / (2.0 * bs * n_row * group)
    dense = n_row <= slots
    kmax = n_row if dense else slots
    r, c, p = lax.axis_index("row"), lax.axis_index("col"), lax.axis_index("pol")
    g = c * n_pol + p

    load = pltpu.make_async_copy(blocks_hbm, blk.at[pl.ds(0, slots)], blk_sem)
    load.start()

    def row_peer(d):
        return {"row": lax.rem(r + d, n_row)}

    def group_peer(e):
        j = lax.rem(g + e, group)
        return j, {"col": lax.div(j, n_pol), "pol": lax.rem(j, n_pol)}

    barrier = pltpu.get_barrier_semaphore()
    for d in range(1, n_row):
        pl.semaphore_signal(barrier, inc=1, device_id=row_peer(d), device_id_type=pl.DeviceIdType.MESH)
    for e in range(1, group):
        pl.semaphore_signal(barrier, inc=1, device_id=group_peer(e)[1], device_id_type=pl.DeviceIdType.MESH)
    pl.semaphore_wait(barrier, n_row - 1 + group - 1)

    def remote(src, dst, send, recv, device):
        return pltpu.make_async_remote_copy(
            src_ref=src, dst_ref=dst, send_sem=send, recv_sem=recv,
            device_id=device, device_id_type=pl.DeviceIdType.MESH,
        )

    gathers = [
        remote(sub_ref, panel.at[d], p_send.at[d], p_recv.at[d], row_peer(d))
        for d in range(1, n_row)
    ]
    for copy in gathers:
        copy.start()

    live = count_ref[0, 0, 0]
    for t in range(group):
        for k in range(kmax):
            if dense:
                slot = jnp.int32(slots)
                for s in range(slots):
                    match = (rows_ref[0, 0, 0, s] == t) & (cols_ref[0, 0, 0, s] == k) & (live > s)
                    slot = jnp.where(match, jnp.int32(s), slot)
            else:
                match = (rows_ref[0, 0, 0, k] == t) & (live > k)
                slot = jnp.where(match, jnp.int32(k), jnp.int32(slots))
            table[t * kmax + k] = slot
    if not dense:
        for k in range(kmax):
            ctable[k] = cols_ref[0, 0, 0, k]
    blk[slots] = jnp.zeros_like(blk[slots])

    def place(q, part):
        real, imag = part[:, :half], part[:, half:]
        weights[q, :bs] = part
        weights[q, bs:] = jnp.concatenate([-imag, real], axis=1)

    place(r, sub_ref[...])
    for d in range(1, n_row):
        gathers[d - 1].wait_recv()
        place(lax.rem(r - d + n_row, n_row), panel[d])
    load.wait()

    def product(t):
        if dense:
            left, right = [], []
            for k in range(kmax):
                slot = table[t * kmax + k]
                left += [blk[slot, 0], blk[slot, 1]]
                right.append(weights[k])
            return jnp.dot(
                jnp.concatenate(left, axis=1), jnp.concatenate(right, axis=0), preferred_element_type=F32
            )
        sums[...] = jnp.zeros_like(sums)

        def add(k, carry):
            slot, col = table[t * kmax + k], ctable[k]
            lhs = jnp.concatenate([blk[slot, 0], blk[slot, 1]], axis=1)
            sums[...] += jnp.dot(lhs, weights[col], preferred_element_type=F32)
            return carry

        lax.fori_loop(0, kmax, add, 0)
        return sums[...]

    def iteration(it, carry):
        firsts, seconds = [], []
        for d in list(range(1, n_col)) + [0]:
            cc = lax.rem(c + d, n_col)
            send1[it, d] = product(cc * n_pol + 1 - p)
            copy = remote(send1.at[it, d], recv1.at[it, d], s1_send.at[it, d], s1_recv.at[it, d], {"pol": 1 - p})
            copy.start()
            firsts.append(copy)
            own1[d] = product(cc * n_pol + p)
            if d:
                copy.wait_recv()
                send2[it, d] = own1[d] + recv1[it, d]
                copy = remote(
                    send2.at[it, d], recv2.at[it, d], s2_send.at[it, d], s2_recv.at[it, d], {"col": cc}
                )
                copy.start()
                seconds.append(copy)
        firsts[-1].wait_recv()
        image = own1[0] + recv1[it, 0]
        for d in range(1, n_col):
            seconds[d - 1].wait_recv()
            image = image + recv2[it, d]
        ybuf[it] = image

        tall = jnp.concatenate([image[:, :half], image[:, half:]], axis=0)
        gram_own[it] = lax.dot_general(
            tall, tall, (((0,), (0,)), ((), ())), precision=HI, preferred_element_type=F32
        )
        stage_a = []
        for e in range(1, group):
            j, device = group_peer(e)
            src = gram_own.at[it, pl.ds(pl.multiple_of(j * chunk, 8), chunk)]
            copy = remote(src, gram_a.at[it, e], a_send.at[it, e], a_recv.at[it, e], device)
            copy.start()
            stage_a.append(copy)
        mine = pl.ds(pl.multiple_of(g * chunk, 8), chunk)
        part = gram_own[it, mine]
        for e in range(1, group):
            stage_a[e - 1].wait_recv()
            part = part + gram_a[it, e]
        gram_sb[it] = part
        gram_b[it, r] = part
        stage_b = []
        for d in range(1, n_row):
            copy = remote(
                gram_sb.at[it], gram_b.at[it, r], b_send.at[it, d], b_recv.at[it, d], row_peer(d)
            )
            copy.start()
            stage_b.append(copy)

        def image_copy(d):
            return remote(ybuf.at[0], ygather.at[d], y_send.at[d], y_recv.at[d], row_peer(d))

        @pl.when(it < ITERS - 1)
        def _():
            for d in range(1, n_row):
                image_copy(d).start()

        for d in range(1, n_row):
            stage_b[d - 1].wait_recv()
        total = gram_b[it, 0]
        for q in range(1, n_row):
            total = total + gram_b[it, q]
        gram_full[it, mine] = total * scale
        stage_c = []
        for e in range(1, group):
            copy = remote(
                gram_full.at[it, mine], gram_full.at[it, mine], c_send.at[it, e], c_recv.at[it, e], group_peer(e)[1]
            )
            copy.start()
            stage_c.append(copy)
        for e in range(1, group):
            back = lax.rem(g - e + group, group)
            theirs = gram_full.at[it, pl.ds(pl.multiple_of(back * chunk, 8), chunk)]
            remote(theirs, theirs, c_send.at[it, e], c_recv.at[it, e], group_peer(e)[1]).wait_recv()

        upper, inverse = factor_and_inverse(gram_full[it])
        turned = inverse.T
        blank = jnp.zeros_like(turned)
        solve = jnp.concatenate(
            [jnp.concatenate([turned, blank], axis=1), jnp.concatenate([blank, turned], axis=1)], axis=0
        )

        def normal(rows):
            return jnp.dot(rows, solve, precision=HI, preferred_element_type=F32)

        @pl.when(it < ITERS - 1)
        def _():
            place(r, normal(ybuf[0]).astype(BF16))
            for d in range(1, n_row):
                image_copy(d).wait()
                place(lax.rem(r - d + n_row, n_row), normal(ygather[d]).astype(BF16))

        @pl.when(it == ITERS - 1)
        def _():
            out_ref[...] = normal(ybuf[ITERS - 1])
            factor_ref[...] = upper.T

        for copy in firsts + seconds + stage_a + stage_b + stage_c:
            copy.wait_send()
        return carry

    lax.fori_loop(0, ITERS, iteration, 0)
    for copy in gathers:
        copy.wait_send()


def on_device(tcc_blocks, slot_rows, slot_cols, slot_count, subspace):
    bs, width = subspace.shape
    half = width // 2
    n_row, n_col, n_pol = lax.axis_size("row"), lax.axis_size("col"), lax.axis_size("pol")
    group = n_col * n_pol
    slots = tcc_blocks.shape[3]
    chunk = half // group
    kmax = n_row if n_row <= slots else slots
    sizes = (n_row, n_col, n_pol, slots, bs, width)
    dma = pltpu.SemaphoreType.DMA
    vmem = pl.BlockSpec(memory_space=pltpu.VMEM)
    smem = pl.BlockSpec(memory_space=pltpu.SMEM)
    return pl.pallas_call(
        functools.partial(kernel, sizes),
        out_shape=(
            jax.ShapeDtypeStruct((bs, width), F32),
            jax.ShapeDtypeStruct((half, half), F32),
        ),
        in_specs=[pl.BlockSpec(memory_space=pl.ANY), smem, smem, smem, vmem],
        out_specs=(vmem, vmem),
        scratch_shapes=[
            pltpu.VMEM((slots + 1, 2, bs, bs), BF16),
            pltpu.VMEM((n_row, bs, width), BF16),
            pltpu.VMEM((n_row, 2 * bs, width), BF16),
            pltpu.SMEM((group * kmax,), jnp.int32),
            pltpu.SMEM((slots,), jnp.int32),
            pltpu.VMEM((bs, width), F32),
            pltpu.VMEM((n_col, bs, width), F32),
            pltpu.VMEM((ITERS, n_col, bs, width), F32),
            pltpu.VMEM((ITERS, n_col, bs, width), F32),
            pltpu.VMEM((ITERS, n_col, bs, width), F32),
            pltpu.VMEM((ITERS, n_col, bs, width), F32),
            pltpu.VMEM((ITERS, bs, width), F32),
            pltpu.VMEM((n_row, bs, width), F32),
            pltpu.VMEM((ITERS, half, half), F32),
            pltpu.VMEM((ITERS, group, chunk, half), F32),
            pltpu.VMEM((ITERS, n_row, chunk, half), F32),
            pltpu.VMEM((ITERS, chunk, half), F32),
            pltpu.VMEM((ITERS, half, half), F32),
            dma,
            dma((n_row,)), dma((n_row,)),
            dma((ITERS, n_col)), dma((ITERS, n_col)),
            dma((ITERS, n_col)), dma((ITERS, n_col)),
            dma((n_row,)), dma((n_row,)),
            dma((ITERS, group)), dma((ITERS, group)),
            dma((ITERS, n_row)), dma((ITERS, n_row)),
            dma((ITERS, group)), dma((ITERS, group)),
        ],
        compiler_params=pltpu.CompilerParams(
            collective_id=0, has_side_effects=True, vmem_limit_bytes=56 * 1024 * 1024
        ),
    )(tcc_blocks.reshape(slots, 2, bs, bs), slot_rows, slot_cols, slot_count, subspace)


def solution(mesh):
    placed = (
        P(("clip", "row"), "col", "pol", None, None, None, None),
        P(("clip", "row"), "col", "pol", None),
        P(("clip", "row"), "col", "pol", None),
        P(("clip", "row"), "col", "pol"),
        P(("clip", "row", "col", "pol"), None),
    )
    return jax.shard_map(
        on_device,
        mesh=mesh,
        in_specs=placed,
        out_specs=(P(("clip", "row", "col", "pol"), None), P("clip", None)),
        check_vma=False,
    )
```

```python
import functools

import jax
import jax.numpy as jnp
from jax import lax
from jax.experimental import pallas as pl
from jax.experimental.pallas import tpu as pltpu
from jax.sharding import PartitionSpec as P

ITERS = 2
F32 = jnp.float32
BF16 = jnp.bfloat16
HI = lax.Precision.HIGHEST
PANEL = 8
EARLY = 128


def factor_and_inverse(gram):
    order = gram.shape[0]
    lane = lax.broadcasted_iota(jnp.int32, (1, order), 1)
    lanes = lax.broadcasted_iota(jnp.int32, (PANEL, order), 1)
    subs = lax.broadcasted_iota(jnp.int32, (PANEL, order), 0)
    upper_rows, inverse_rows = [], []
    rest = gram
    for start in range(0, order, PANEL):
        top, rest = rest[:PANEL], rest[PANEL:]
        left = order - start - PANEL
        diag = [jnp.broadcast_to(top[:, start + k:start + k + 1], (PANEL, order)) for k in range(PANEL)]
        if left:
            below = [jnp.broadcast_to(rest[:, start + k:start + k + 1], (left, order)) for k in range(PANEL)]
            rest = jnp.where((lane >= start) & (lane < start + PANEL), 0.0, rest)
        pivots = diag[0]
        for k in range(PANEL):
            here = start + k
            inv = 1.0 / diag[k][k:k + 1]
            under = jnp.where(subs > k, diag[k], 0.0)
            mults = {l: diag[l][k:k + 1] * inv for l in range(k + 1, PANEL)}
            row = jnp.where(lane == here, 1.0, top[k:k + 1]) * inv
            if k:
                pivots = jnp.where(subs == k, diag[k], pivots)
            top = jnp.where((lanes == here) & (subs > k), 0.0, top) - under * row
            for l in range(k + 1, PANEL):
                diag[l] = diag[l] - under * mults[l]
            if left:
                row = jnp.where((lane > here) & (lane < start + PANEL), 0.0, row)
                rest = rest - below[k] * row
                for l in range(k + 1, PANEL):
                    below[l] = below[l] - below[k] * mults[l]
        root = lax.rsqrt(pivots)
        scaled = top * root
        upper_rows.append(jnp.where(lanes >= subs + start, scaled, 0.0))
        inverse_rows.append(jnp.where(lanes < subs + start, scaled, jnp.where(lanes == subs + start, root, 0.0)))
    return jnp.concatenate(upper_rows, axis=0), jnp.concatenate(inverse_rows, axis=0)


def kernel(
    sizes,
    blocks_hbm, rows_ref, cols_ref, count_ref, sub_ref,
    out_ref, factor_ref,
    blk, panel, weights, table, ctable, sums, own1, send1, recv1, send2, recv2, ybuf, ygather, xbuf, late,
    gram_own, gram_a, gram_b, gram_sb, gram_full,
    blk_sem, p_send, p_recv, s1_send, s1_recv, s2_send, s2_recv, y_send, y_recv, x_send, x_recv,
    a_send, a_recv, b_send, b_recv, c_send, c_recv,
):
    n_row, n_col, n_pol, slots, bs, width = sizes
    half = width // 2
    group = n_col * n_pol
    chunk = half // group
    early = EARLY
    scale = 1.0 / (2.0 * bs * n_row * group)
    dense = n_row <= slots
    kmax = n_row if dense else slots
    r, c, p = lax.axis_index("row"), lax.axis_index("col"), lax.axis_index("pol")
    g = c * n_pol + p

    load = pltpu.make_async_copy(blocks_hbm, blk.at[pl.ds(0, slots)], blk_sem)
    load.start()

    def row_peer(d):
        return {"row": lax.rem(r + d, n_row)}

    def group_peer(e):
        j = lax.rem(g + e, group)
        return j, {"col": lax.div(j, n_pol), "pol": lax.rem(j, n_pol)}

    barrier = pltpu.get_barrier_semaphore()
    for d in range(1, n_row):
        pl.semaphore_signal(barrier, inc=1, device_id=row_peer(d), device_id_type=pl.DeviceIdType.MESH)
    for e in range(1, group):
        pl.semaphore_signal(barrier, inc=1, device_id=group_peer(e)[1], device_id_type=pl.DeviceIdType.MESH)
    pl.semaphore_wait(barrier, n_row - 1 + group - 1)

    def remote(src, dst, send, recv, device):
        return pltpu.make_async_remote_copy(
            src_ref=src, dst_ref=dst, send_sem=send, recv_sem=recv,
            device_id=device, device_id_type=pl.DeviceIdType.MESH,
        )

    class Exchange:
        def __init__(self, src, dst, send, recv):
            self.copies = {
                d: remote(src, dst.at[d], send.at[d], recv.at[d], row_peer(d)) for d in range(1, n_row)
            }

        def start(self):
            for copy in self.copies.values():
                copy.start()

        def wait_recv(self, d):
            self.copies[d].wait_recv()

        def wait_send(self):
            for copy in self.copies.values():
                copy.wait_send()

    first = Exchange(sub_ref, panel, p_send, p_recv)
    first.start()

    live = count_ref[0, 0, 0]
    for t in range(group):
        for k in range(kmax):
            if dense:
                slot = jnp.int32(slots)
                for s in range(slots):
                    match = (rows_ref[0, 0, 0, s] == t) & (cols_ref[0, 0, 0, s] == k) & (live > s)
                    slot = jnp.where(match, jnp.int32(s), slot)
            else:
                match = (rows_ref[0, 0, 0, k] == t) & (live > k)
                slot = jnp.where(match, jnp.int32(k), jnp.int32(slots))
            table[t * kmax + k] = slot
    if not dense:
        for k in range(kmax):
            ctable[k] = cols_ref[0, 0, 0, k]
    blk[slots] = jnp.zeros_like(blk[slots])

    def place(q, part, low=0):
        real, imag = part[:, :half], part[:, half:]
        count = part.shape[0]
        weights[q, low:low + count] = part
        weights[q, bs + low:bs + low + count] = jnp.concatenate([-imag, real], axis=1)

    place(r, sub_ref[...])
    for d in range(1, n_row):
        first.wait_recv(d)
        place(lax.rem(r - d + n_row, n_row), panel[d])
    load.wait()
    image_part = Exchange(ybuf.at[0, pl.ds(0, early)], ygather, y_send, y_recv)
    late_part = Exchange(xbuf.at[pl.ds(early, bs - early)], late, x_send, x_recv)

    def product(t):
        if dense:
            left, right = [], []
            for k in range(kmax):
                slot = table[t * kmax + k]
                left += [blk[slot, 0], blk[slot, 1]]
                right.append(weights[k])
            return jnp.dot(
                jnp.concatenate(left, axis=1), jnp.concatenate(right, axis=0), preferred_element_type=F32
            )
        sums[...] = jnp.zeros_like(sums)

        def add(k, carry):
            slot, col = table[t * kmax + k], ctable[k]
            lhs = jnp.concatenate([blk[slot, 0], blk[slot, 1]], axis=1)
            sums[...] += jnp.dot(lhs, weights[col], preferred_element_type=F32)
            return carry

        lax.fori_loop(0, kmax, add, 0)
        return sums[...]

    def iteration(it, carry):
        firsts, seconds = [], []
        for d in list(range(1, n_col)) + [0]:
            cc = lax.rem(c + d, n_col)
            send1[it, d] = product(cc * n_pol + 1 - p)
            copy = remote(send1.at[it, d], recv1.at[it, d], s1_send.at[it, d], s1_recv.at[it, d], {"pol": 1 - p})
            copy.start()
            firsts.append(copy)
            own1[d] = product(cc * n_pol + p)
            if d:
                copy.wait_recv()
                send2[it, d] = own1[d] + recv1[it, d]
                copy = remote(
                    send2.at[it, d], recv2.at[it, d], s2_send.at[it, d], s2_recv.at[it, d], {"col": cc}
                )
                copy.start()
                seconds.append(copy)
        firsts[-1].wait_recv()
        image = own1[0] + recv1[it, 0]
        for d in range(1, n_col):
            seconds[d - 1].wait_recv()
            image = image + recv2[it, d]
        ybuf[it] = image

        tall = jnp.concatenate([image[:, :half], image[:, half:]], axis=0)
        gram_own[it] = lax.dot_general(
            tall, tall, (((0,), (0,)), ((), ())), precision=HI, preferred_element_type=F32
        )
        stage_a = []
        for e in range(1, group):
            j, device = group_peer(e)
            src = gram_own.at[it, pl.ds(pl.multiple_of(j * chunk, 8), chunk)]
            copy = remote(src, gram_a.at[it, e], a_send.at[it, e], a_recv.at[it, e], device)
            copy.start()
            stage_a.append(copy)
        mine = pl.ds(pl.multiple_of(g * chunk, 8), chunk)
        part = gram_own[it, mine]
        for e in range(1, group):
            stage_a[e - 1].wait_recv()
            part = part + gram_a[it, e]
        stage_b = []
        gram_sb[it] = part
        gram_b[it, r] = part
        for d in range(1, n_row):
            copy = remote(
                gram_sb.at[it], gram_b.at[it, r], b_send.at[it, d], b_recv.at[it, d], row_peer(d)
            )
            copy.start()
            stage_b.append(copy)
        @pl.when(it < ITERS - 1)
        def _():
            image_part.start()

        for copy in stage_b:
            copy.wait_recv()
        part = gram_b[it, 0]
        for q in range(1, n_row):
            part = part + gram_b[it, q]
        gram_full[it, mine] = part * scale
        stage_c = []
        for e in range(1, group):
            copy = remote(
                gram_full.at[it, mine], gram_full.at[it, mine], c_send.at[it, e], c_recv.at[it, e], group_peer(e)[1]
            )
            copy.start()
            stage_c.append(copy)
        for e in range(1, group):
            back = lax.rem(g - e + group, group)
            theirs = gram_full.at[it, pl.ds(pl.multiple_of(back * chunk, 8), chunk)]
            remote(theirs, theirs, c_send.at[it, e], c_recv.at[it, e], group_peer(e)[1]).wait_recv()

        upper, inverse = factor_and_inverse(gram_full[it])
        turned = inverse.T
        blank = jnp.zeros_like(turned)
        solve = jnp.concatenate(
            [jnp.concatenate([turned, blank], axis=1), jnp.concatenate([blank, turned], axis=1)], axis=0
        )

        def normal(rows):
            return jnp.dot(rows, solve, precision=HI, preferred_element_type=F32)

        @pl.when(it < ITERS - 1)
        def _():
            xbuf[...] = normal(ybuf[0]).astype(BF16)
            late_part.start()
            place(r, xbuf[...])
            for d in range(1, n_row):
                image_part.wait_recv(d)
                place(lax.rem(r - d + n_row, n_row), normal(ygather[d]).astype(BF16))
            for d in range(1, n_row):
                late_part.wait_recv(d)
                place(lax.rem(r - d + n_row, n_row), late[d], early)
            image_part.wait_send()
            late_part.wait_send()

        @pl.when(it == ITERS - 1)
        def _():
            out_ref[...] = normal(ybuf[ITERS - 1])
            factor_ref[...] = upper.T

        for copy in firsts + seconds + stage_a + stage_b + stage_c:
            copy.wait_send()
        return carry

    lax.fori_loop(0, ITERS, iteration, 0)
    first.wait_send()


def on_device(tcc_blocks, slot_rows, slot_cols, slot_count, subspace):
    bs, width = subspace.shape
    half = width // 2
    n_row, n_col, n_pol = lax.axis_size("row"), lax.axis_size("col"), lax.axis_size("pol")
    group = n_col * n_pol
    slots = tcc_blocks.shape[3]
    chunk = half // group
    kmax = n_row if n_row <= slots else slots
    sizes = (n_row, n_col, n_pol, slots, bs, width)
    dma = pltpu.SemaphoreType.DMA
    vmem = pl.BlockSpec(memory_space=pltpu.VMEM)
    smem = pl.BlockSpec(memory_space=pltpu.SMEM)
    return pl.pallas_call(
        functools.partial(kernel, sizes),
        out_shape=(
            jax.ShapeDtypeStruct((bs, width), F32),
            jax.ShapeDtypeStruct((half, half), F32),
        ),
        in_specs=[pl.BlockSpec(memory_space=pl.ANY), smem, smem, smem, vmem],
        out_specs=(vmem, vmem),
        scratch_shapes=[
            pltpu.VMEM((slots + 1, 2, bs, bs), BF16),
            pltpu.VMEM((n_row, bs, width), BF16),
            pltpu.VMEM((n_row, 2 * bs, width), BF16),
            pltpu.SMEM((group * kmax,), jnp.int32),
            pltpu.SMEM((slots,), jnp.int32),
            pltpu.VMEM((bs, width), F32),
            pltpu.VMEM((n_col, bs, width), F32),
            pltpu.VMEM((ITERS, n_col, bs, width), F32),
            pltpu.VMEM((ITERS, n_col, bs, width), F32),
            pltpu.VMEM((ITERS, n_col, bs, width), F32),
            pltpu.VMEM((ITERS, n_col, bs, width), F32),
            pltpu.VMEM((ITERS, bs, width), F32),
            pltpu.VMEM((n_row, EARLY, width), F32),
            pltpu.VMEM((bs, width), BF16),
            pltpu.VMEM((n_row, bs - EARLY, width), BF16),
            pltpu.VMEM((ITERS, half, half), F32),
            pltpu.VMEM((ITERS, group, chunk, half), F32),
            pltpu.VMEM((ITERS, n_row, chunk, half), F32),
            pltpu.VMEM((ITERS, chunk, half), F32),
            pltpu.VMEM((ITERS, half, half), F32),
            dma,
            dma((n_row,)), dma((n_row,)),
            dma((ITERS, n_col)), dma((ITERS, n_col)),
            dma((ITERS, n_col)), dma((ITERS, n_col)),
            dma((n_row,)), dma((n_row,)),
            dma((n_row,)), dma((n_row,)),
            dma((ITERS, group)), dma((ITERS, group)),
            dma((ITERS, n_row)), dma((ITERS, n_row)),
            dma((ITERS, group)), dma((ITERS, group)),
        ],
        compiler_params=pltpu.CompilerParams(
            collective_id=0, has_side_effects=True, vmem_limit_bytes=56 * 1024 * 1024
        ),
    )(tcc_blocks.reshape(slots, 2, bs, bs), slot_rows, slot_cols, slot_count, subspace)


def solution(mesh):
    placed = (
        P(("clip", "row"), "col", "pol", None, None, None, None),
        P(("clip", "row"), "col", "pol", None),
        P(("clip", "row"), "col", "pol", None),
        P(("clip", "row"), "col", "pol"),
        P(("clip", "row", "col", "pol"), None),
    )
    return jax.shard_map(
        on_device,
        mesh=mesh,
        in_specs=placed,
        out_specs=(P(("clip", "row", "col", "pol"), None), P("clip", None)),
        check_vma=False,
    )
```

```python
import functools

import jax
import jax.numpy as jnp
from jax import lax
from jax.experimental import pallas as pl
from jax.experimental.pallas import tpu as pltpu
from jax.sharding import PartitionSpec as P

ITERS = 2
F32 = jnp.float32
BF16 = jnp.bfloat16
HI = lax.Precision.HIGHEST
PANEL = 8
EARLY = 96


def factor_and_inverse(gram):
    order = gram.shape[0]
    lane = lax.broadcasted_iota(jnp.int32, (1, order), 1)
    lanes = lax.broadcasted_iota(jnp.int32, (PANEL, order), 1)
    subs = lax.broadcasted_iota(jnp.int32, (PANEL, order), 0)
    upper_rows, inverse_rows = [], []
    rest = gram
    for start in range(0, order, PANEL):
        top, rest = rest[:PANEL], rest[PANEL:]
        left = order - start - PANEL
        diag = [jnp.broadcast_to(top[:, start + k:start + k + 1], (PANEL, order)) for k in range(PANEL)]
        if left:
            below = [jnp.broadcast_to(rest[:, start + k:start + k + 1], (left, order)) for k in range(PANEL)]
            rest = jnp.where((lane >= start) & (lane < start + PANEL), 0.0, rest)
        pivots = diag[0]
        for k in range(PANEL):
            here = start + k
            inv = 1.0 / diag[k][k:k + 1]
            under = jnp.where(subs > k, diag[k], 0.0)
            mults = {l: diag[l][k:k + 1] * inv for l in range(k + 1, PANEL)}
            row = jnp.where(lane == here, 1.0, top[k:k + 1]) * inv
            if k:
                pivots = jnp.where(subs == k, diag[k], pivots)
            top = jnp.where((lanes == here) & (subs > k), 0.0, top) - under * row
            for l in range(k + 1, PANEL):
                diag[l] = diag[l] - under * mults[l]
            if left:
                row = jnp.where((lane > here) & (lane < start + PANEL), 0.0, row)
                rest = rest - below[k] * row
                for l in range(k + 1, PANEL):
                    below[l] = below[l] - below[k] * mults[l]
        root = lax.rsqrt(pivots)
        scaled = top * root
        upper_rows.append(jnp.where(lanes >= subs + start, scaled, 0.0))
        inverse_rows.append(jnp.where(lanes < subs + start, scaled, jnp.where(lanes == subs + start, root, 0.0)))
    return jnp.concatenate(upper_rows, axis=0), jnp.concatenate(inverse_rows, axis=0)


def kernel(
    sizes,
    blocks_hbm, rows_ref, cols_ref, count_ref, sub_ref,
    out_ref, factor_ref,
    blk, panel, weights, table, ctable, sums, own1, send1, recv1, send2, recv2, ybuf, ygather, xbuf, late,
    gram_own, gram_a, gram_b, gram_sb, gram_full,
    blk_sem, p_send, p_recv, s1_send, s1_recv, s2_send, s2_recv, y_send, y_recv, x_send, x_recv,
    a_send, a_recv, b_send, b_recv, c_send, c_recv,
):
    n_row, n_col, n_pol, slots, bs, width = sizes
    half = width // 2
    group = n_col * n_pol
    chunk = half // group
    early = EARLY
    scale = 1.0 / (2.0 * bs * n_row * group)
    dense = n_row <= slots
    kmax = n_row if dense else slots
    r, c, p = lax.axis_index("row"), lax.axis_index("col"), lax.axis_index("pol")
    g = c * n_pol + p

    load = pltpu.make_async_copy(blocks_hbm, blk.at[pl.ds(0, slots)], blk_sem)
    load.start()

    def row_peer(d):
        return {"row": lax.rem(r + d, n_row)}

    def group_peer(e):
        j = lax.rem(g + e, group)
        return j, {"col": lax.div(j, n_pol), "pol": lax.rem(j, n_pol)}

    barrier = pltpu.get_barrier_semaphore()
    for d in range(1, n_row):
        pl.semaphore_signal(barrier, inc=1, device_id=row_peer(d), device_id_type=pl.DeviceIdType.MESH)
    for e in range(1, group):
        pl.semaphore_signal(barrier, inc=1, device_id=group_peer(e)[1], device_id_type=pl.DeviceIdType.MESH)
    pl.semaphore_wait(barrier, n_row - 1 + group - 1)

    def remote(src, dst, send, recv, device):
        return pltpu.make_async_remote_copy(
            src_ref=src, dst_ref=dst, send_sem=send, recv_sem=recv,
            device_id=device, device_id_type=pl.DeviceIdType.MESH,
        )

    class Exchange:
        def __init__(self, src, dst, send, recv):
            self.copies = {
                d: remote(src, dst.at[d], send.at[d], recv.at[d], row_peer(d)) for d in range(1, n_row)
            }

        def start(self):
            for copy in self.copies.values():
                copy.start()

        def wait_recv(self, d):
            self.copies[d].wait_recv()

        def wait_send(self):
            for copy in self.copies.values():
                copy.wait_send()

    first = Exchange(sub_ref, panel, p_send, p_recv)
    first.start()

    live = count_ref[0, 0, 0]
    for t in range(group):
        for k in range(kmax):
            if dense:
                slot = jnp.int32(slots)
                for s in range(slots):
                    match = (rows_ref[0, 0, 0, s] == t) & (cols_ref[0, 0, 0, s] == k) & (live > s)
                    slot = jnp.where(match, jnp.int32(s), slot)
            else:
                match = (rows_ref[0, 0, 0, k] == t) & (live > k)
                slot = jnp.where(match, jnp.int32(k), jnp.int32(slots))
            table[t * kmax + k] = slot
    if not dense:
        for k in range(kmax):
            ctable[k] = cols_ref[0, 0, 0, k]
    blk[slots] = jnp.zeros_like(blk[slots])

    def place(q, part, low=0):
        real, imag = part[:, :half], part[:, half:]
        count = part.shape[0]
        weights[q, low:low + count] = part
        weights[q, bs + low:bs + low + count] = jnp.concatenate([-imag, real], axis=1)

    place(r, sub_ref[...])
    for d in range(1, n_row):
        first.wait_recv(d)
        place(lax.rem(r - d + n_row, n_row), panel[d])
    load.wait()
    image_part = Exchange(ybuf.at[0, pl.ds(0, early)], ygather, y_send, y_recv)
    late_part = Exchange(xbuf.at[pl.ds(early, bs - early)], late, x_send, x_recv)

    def product(t):
        if dense:
            left, right = [], []
            for k in range(kmax):
                slot = table[t * kmax + k]
                left += [blk[slot, 0], blk[slot, 1]]
                right.append(weights[k])
            return jnp.dot(
                jnp.concatenate(left, axis=1), jnp.concatenate(right, axis=0), preferred_element_type=F32
            )
        sums[...] = jnp.zeros_like(sums)

        def add(k, carry):
            slot, col = table[t * kmax + k], ctable[k]
            lhs = jnp.concatenate([blk[slot, 0], blk[slot, 1]], axis=1)
            sums[...] += jnp.dot(lhs, weights[col], preferred_element_type=F32)
            return carry

        lax.fori_loop(0, kmax, add, 0)
        return sums[...]

    def iteration(it, carry):
        firsts, seconds = [], []
        for d in list(range(1, n_col)) + [0]:
            cc = lax.rem(c + d, n_col)
            send1[it, d] = product(cc * n_pol + 1 - p)
            copy = remote(send1.at[it, d], recv1.at[it, d], s1_send.at[it, d], s1_recv.at[it, d], {"pol": 1 - p})
            copy.start()
            firsts.append(copy)
            own1[d] = product(cc * n_pol + p)
            if d:
                copy.wait_recv()
                send2[it, d] = own1[d] + recv1[it, d]
                copy = remote(
                    send2.at[it, d], recv2.at[it, d], s2_send.at[it, d], s2_recv.at[it, d], {"col": cc}
                )
                copy.start()
                seconds.append(copy)
        firsts[-1].wait_recv()
        image = own1[0] + recv1[it, 0]
        for d in range(1, n_col):
            seconds[d - 1].wait_recv()
            image = image + recv2[it, d]
        ybuf[it] = image

        tall = jnp.concatenate([image[:, :half], image[:, half:]], axis=0)
        gram_own[it] = lax.dot_general(
            tall, tall, (((0,), (0,)), ((), ())), precision=HI, preferred_element_type=F32
        )
        stage_a = []
        for e in range(1, group):
            j, device = group_peer(e)
            src = gram_own.at[it, pl.ds(pl.multiple_of(j * chunk, 8), chunk)]
            copy = remote(src, gram_a.at[it, e], a_send.at[it, e], a_recv.at[it, e], device)
            copy.start()
            stage_a.append(copy)
        mine = pl.ds(pl.multiple_of(g * chunk, 8), chunk)
        part = gram_own[it, mine]
        for e in range(1, group):
            stage_a[e - 1].wait_recv()
            part = part + gram_a[it, e]
        stage_b = []
        gram_sb[it] = part
        gram_b[it, r] = part
        for d in range(1, n_row):
            copy = remote(
                gram_sb.at[it], gram_b.at[it, r], b_send.at[it, d], b_recv.at[it, d], row_peer(d)
            )
            copy.start()
            stage_b.append(copy)
        @pl.when(it < ITERS - 1)
        def _():
            image_part.start()

        for copy in stage_b:
            copy.wait_recv()
        part = gram_b[it, 0]
        for q in range(1, n_row):
            part = part + gram_b[it, q]
        gram_full[it, mine] = part * scale
        stage_c = []
        for e in range(1, group):
            copy = remote(
                gram_full.at[it, mine], gram_full.at[it, mine], c_send.at[it, e], c_recv.at[it, e], group_peer(e)[1]
            )
            copy.start()
            stage_c.append(copy)
        for e in range(1, group):
            back = lax.rem(g - e + group, group)
            theirs = gram_full.at[it, pl.ds(pl.multiple_of(back * chunk, 8), chunk)]
            remote(theirs, theirs, c_send.at[it, e], c_recv.at[it, e], group_peer(e)[1]).wait_recv()

        upper, inverse = factor_and_inverse(gram_full[it])
        turned = inverse.T
        blank = jnp.zeros_like(turned)
        solve = jnp.concatenate(
            [jnp.concatenate([turned, blank], axis=1), jnp.concatenate([blank, turned], axis=1)], axis=0
        )

        def normal(rows):
            return jnp.dot(rows, solve, precision=HI, preferred_element_type=F32)

        @pl.when(it < ITERS - 1)
        def _():
            xbuf[early:] = normal(ybuf[0, early:]).astype(BF16)
            late_part.start()
            xbuf[:early] = normal(ybuf[0, :early]).astype(BF16)
            place(r, xbuf[...])
            for d in range(1, n_row):
                image_part.wait_recv(d)
                place(lax.rem(r - d + n_row, n_row), normal(ygather[d]).astype(BF16))
            for d in range(1, n_row):
                late_part.wait_recv(d)
                place(lax.rem(r - d + n_row, n_row), late[d], early)
            image_part.wait_send()
            late_part.wait_send()

        @pl.when(it == ITERS - 1)
        def _():
            out_ref[...] = normal(ybuf[ITERS - 1])
            factor_ref[...] = upper.T

        for copy in firsts + seconds + stage_a + stage_b + stage_c:
            copy.wait_send()
        return carry

    lax.fori_loop(0, ITERS, iteration, 0)
    first.wait_send()


def on_device(tcc_blocks, slot_rows, slot_cols, slot_count, subspace):
    bs, width = subspace.shape
    half = width // 2
    n_row, n_col, n_pol = lax.axis_size("row"), lax.axis_size("col"), lax.axis_size("pol")
    group = n_col * n_pol
    slots = tcc_blocks.shape[3]
    chunk = half // group
    kmax = n_row if n_row <= slots else slots
    sizes = (n_row, n_col, n_pol, slots, bs, width)
    dma = pltpu.SemaphoreType.DMA
    vmem = pl.BlockSpec(memory_space=pltpu.VMEM)
    smem = pl.BlockSpec(memory_space=pltpu.SMEM)
    return pl.pallas_call(
        functools.partial(kernel, sizes),
        out_shape=(
            jax.ShapeDtypeStruct((bs, width), F32),
            jax.ShapeDtypeStruct((half, half), F32),
        ),
        in_specs=[pl.BlockSpec(memory_space=pl.ANY), smem, smem, smem, vmem],
        out_specs=(vmem, vmem),
        scratch_shapes=[
            pltpu.VMEM((slots + 1, 2, bs, bs), BF16),
            pltpu.VMEM((n_row, bs, width), BF16),
            pltpu.VMEM((n_row, 2 * bs, width), BF16),
            pltpu.SMEM((group * kmax,), jnp.int32),
            pltpu.SMEM((slots,), jnp.int32),
            pltpu.VMEM((bs, width), F32),
            pltpu.VMEM((n_col, bs, width), F32),
            pltpu.VMEM((ITERS, n_col, bs, width), F32),
            pltpu.VMEM((ITERS, n_col, bs, width), F32),
            pltpu.VMEM((ITERS, n_col, bs, width), F32),
            pltpu.VMEM((ITERS, n_col, bs, width), F32),
            pltpu.VMEM((ITERS, bs, width), F32),
            pltpu.VMEM((n_row, EARLY, width), F32),
            pltpu.VMEM((bs, width), BF16),
            pltpu.VMEM((n_row, bs - EARLY, width), BF16),
            pltpu.VMEM((ITERS, half, half), F32),
            pltpu.VMEM((ITERS, group, chunk, half), F32),
            pltpu.VMEM((ITERS, n_row, chunk, half), F32),
            pltpu.VMEM((ITERS, chunk, half), F32),
            pltpu.VMEM((ITERS, half, half), F32),
            dma,
            dma((n_row,)), dma((n_row,)),
            dma((ITERS, n_col)), dma((ITERS, n_col)),
            dma((ITERS, n_col)), dma((ITERS, n_col)),
            dma((n_row,)), dma((n_row,)),
            dma((n_row,)), dma((n_row,)),
            dma((ITERS, group)), dma((ITERS, group)),
            dma((ITERS, n_row)), dma((ITERS, n_row)),
            dma((ITERS, group)), dma((ITERS, group)),
        ],
        compiler_params=pltpu.CompilerParams(
            collective_id=0, has_side_effects=True, vmem_limit_bytes=56 * 1024 * 1024
        ),
    )(tcc_blocks.reshape(slots, 2, bs, bs), slot_rows, slot_cols, slot_count, subspace)


def solution(mesh):
    placed = (
        P(("clip", "row"), "col", "pol", None, None, None, None),
        P(("clip", "row"), "col", "pol", None),
        P(("clip", "row"), "col", "pol", None),
        P(("clip", "row"), "col", "pol"),
        P(("clip", "row", "col", "pol"), None),
    )
    return jax.shard_map(
        on_device,
        mesh=mesh,
        in_specs=placed,
        out_specs=(P(("clip", "row", "col", "pol"), None), P("clip", None)),
        check_vma=False,
    )
```
